32 devices in a mesh: lon: 8 (over z, x), grp: 4 (over y, core).
Axes of the slice: x: 2, y: 2, z: 4, core: 2. Of those that a mesh axis runs over, the one named last changes fastest.
Arguments:
- ray_weights: bfloat16 [16384, 128], P(('lon', 'grp')), may hold values from 0.049804688 to 0.44921875
- ray_sector: int32 [16384, 1], P(('lon', 'grp')), may hold values from 0 to 7; in each aligned block of 512 rows (0 to 511, 512 to 1023, ...) at most 128 rows name the same one
- ray_block: int32 [16384], P(('lon', 'grp')), may hold values from 0 to 1023
- ray_offset: int32 [16384], P(('lon', 'grp')), may hold values from 0 to 384
- ray_resid: float32 [16384], P(('lon', 'grp')), may hold values from -6 to 6
- smooth_resid: float32 [16, 512, 512], P('lon'), may hold values from -6 to 6
- model_dir: float32 [16, 512, 512], P('lon'), may hold values from -6 to 6
- search_dir: float32 [16, 512, 512], P('lon'), may hold values from -6 to 6
- model: float32 [16, 512, 512], P('lon'), may hold values from -6 to 6
- stencil_coeffs: float32 [4], replicated, may hold values from 0.05 to 0.3
- lsqr_scalars: float32 [3], replicated, may hold values from 0.5 to 2
Outputs:
- model_new: float32 [16, 512, 512], P('lon')
- search_new: float32 [16, 512, 512], P('lon')
- dir_new: float32 [16, 512, 512], P('lon')
- ray_resid_new: float32 [16384], P(('lon', 'grp'))
- smooth_resid_new: float32 [16, 512, 512], P('lon')
- scalars_new: float32 [4], replicated
The draws below stay inside these ranges and needn't reach their ends.
Inputs may be any that keep to these rules, and one draw needn't show every extreme that they name: `ray_sector`: the rays of one device name one sector at most 128 times, a bound that some block reaches.
All inputs are finite; a program needn't handle non-finite values.
Results may differ from the reference program's by a relative error of at most 0.00095.
Values may be sent and summed in bfloat16 or wider, within the bound.
A program may use at most 64 MiB of HBM per device.

```python
import math
import jax
import jax.numpy as jnp
import numpy as np
from jax import lax

LON_DEV = 2
NLAT = 512
NDEP = 512
BAND = 128
RAY_DEV = 512
CAP = 128
NLON = 16
RAYS = 16384
CELLS = 4194304
N_LON = 8


def set_ends(drawn, rng, low, high):
    spot = [jax.random.randint(jax.random.fold_in(rng, axis), (), 0, length) for axis, length in enumerate(drawn.shape)]
    main_axis = drawn.shape.index(max(drawn.shape))
    neighbour = spot[:main_axis] + [(spot[main_axis] + 1) % drawn.shape[main_axis]] + spot[main_axis + 1:]
    return drawn.at[tuple(spot)].set(low).at[tuple(neighbour)].set(high)


def level_of(own_key, shape, pieces, smallest, high):
    loudness = 1.0
    for position, shards_of in pieces:
        steps = jax.random.uniform(jax.random.fold_in(jax.random.fold_in(own_key, 6), position), (shards_of,), jnp.float32, smallest / len(pieces), high / len(pieces))
        loudness = loudness * jnp.repeat(jnp.exp(steps), shape[position] // shards_of).reshape((-1,) + (1,) * (len(shape) - 1 - position))
    return loudness


def assign_block(own_key, own, number, rows, number_of, top, most, lean):
    ranking = jax.random.permutation(own_key, number_of)
    heavy_load, ordinary = shares(number_of, rows * top, most, lean, True), shares(number_of, rows * top, most, lean, False)
    places = jnp.arange(number_of)

    def named(tallies, offset_by):
        used = int((tallies > 0).sum())
        fixed = max(1, used // 4)
        shifted = fixed + (places - fixed + offset_by * (used - fixed)) % max(1, number_of - fixed)
        return jnp.zeros((number_of,), jnp.int32).at[ranking[jnp.where(places < fixed, places, shifted)]].set(jnp.asarray(tallies, jnp.int32))

    tallies = jnp.where(number % 4 == 0, named(heavy_load, number // 4), named(ordinary, number - number // 4 - 1))
    mixed = jax.random.permutation(jax.random.fold_in(own, 3), number_of)
    donor, taker = mixed[0:number_of // 2 * 2:2], mixed[1:number_of // 2 * 2:2]
    slack = jnp.minimum(tallies[donor] - 1, most - tallies[taker]) // 2
    slack = jnp.where((donor == ranking[0]) | (taker == ranking[0]) | (tallies[taker] == 0), 0, jnp.maximum(slack, 0))
    shifted = jax.random.randint(jax.random.fold_in(own, 4), (number_of // 2,), 0, 1 << 20) % (slack + 1)
    tallies = tallies.at[donor].add(-shifted).at[taker].add(shifted)
    items = jnp.searchsorted(jnp.cumsum(tallies), jnp.arange(rows * top), side="right").astype(jnp.int32)
    listing = items.reshape(top, rows).T
    listing = listing[jax.random.permutation(jax.random.fold_in(own, 1), rows)]
    offset_by = jax.random.randint(jax.random.fold_in(own, 2), (rows, 1), 0, top)
    return jnp.take_along_axis(listing, (jnp.arange(top)[None, :] + offset_by) % top, axis=1)


def shares(count, total, most, skew, full):
    portions = [(1 << 20) // math.isqrt(rank ** skew) + 1 for rank in range(1, count + 1)]
    largest = most if full else min(most, max(-(-total // count), total * portions[0] // sum(portions)))
    least = 1 if total - largest >= count - 1 else 0
    holding, spare = [largest] + [least] * (count - 1), total - largest - least * (count - 1)
    while spare > 0:
        candidates = [i for i in range(1, count) if holding[i] < largest] or [i for i in range(1, count) if holding[i] < most]
        pool, remaining = sum([portions[i] for i in candidates]), spare
        for i in candidates:
            extra = min(most - holding[i], max(1, remaining * portions[i] // pool), spare)
            holding[i] = holding[i] + extra
            spare = spare - extra
    return np.array(holding)


def normal_values(key, shape, spread, most, pieces=(), held_as=jnp.bfloat16):
    drawn = jax.random.normal(key, shape, jnp.float32) * spread
    if len(pieces) > 0:
        drawn = level_of(key, shape, pieces, -0.22, 0.18) * drawn
    return jnp.clip(drawn, min=-most, max=most).astype(held_as)


def setup_inputs(seed: int = 0) -> dict:
    arg_keys = jax.random.split(jax.random.key(seed), 12)
    ray_weights = jnp.clip(0.049804688 + 0.39941406 * jax.random.uniform(arg_keys[0], (RAYS, BAND), jnp.float32) ** level_of(arg_keys[0], (RAYS, BAND), ((0, 32),), -0.2, 0.2), 0.049804688, 0.44921875).astype(jnp.bfloat16)
    ray_sector_keys = jax.random.split(jax.random.fold_in(arg_keys[1], 1), RAYS // RAY_DEV)
    ray_sector_turns = jax.random.permutation(jax.random.fold_in(arg_keys[1], 3), RAYS // RAY_DEV)
    ray_sector = jax.vmap(lambda own, number: assign_block(jax.random.fold_in(arg_keys[1], 2), own, number, RAY_DEV, N_LON, 1, CAP, 2))(ray_sector_keys, ray_sector_turns).reshape((RAYS, 1))
    ray_block = set_ends(jax.random.randint(arg_keys[2], (RAYS,), 0, LON_DEV * NLAT), jax.random.fold_in(arg_keys[2], 1), 0, (LON_DEV * NLAT) - 1).astype(jnp.int32)
    ray_offset = set_ends(jax.random.randint(arg_keys[3], (RAYS,), 0, NDEP - BAND + 1), jax.random.fold_in(arg_keys[3], 1), 0, NDEP - BAND).astype(jnp.int32)
    ray_resid = normal_values(arg_keys[4], (RAYS,), 1.0, 6.0, ((0, 32),), jnp.float32)
    smooth_resid = normal_values(arg_keys[5], (NLON, NLAT, NDEP), 1.0, 6.0, ((0, 8),), jnp.float32)
    model_dir = normal_values(arg_keys[6], (NLON, NLAT, NDEP), 1.0, 6.0, ((0, 8),), jnp.float32)
    search_dir = normal_values(arg_keys[7], (NLON, NLAT, NDEP), 1.0, 6.0, ((0, 8),), jnp.float32)
    model = normal_values(arg_keys[8], (NLON, NLAT, NDEP), 1.0, 6.0, ((0, 8),), jnp.float32)
    stencil_coeffs = jnp.clip(jnp.exp(jax.random.uniform(arg_keys[9], (4,), jnp.float32, math.log(0.05), math.log(0.3))), 0.05, 0.3)
    lsqr_scalars = jnp.clip(jax.random.uniform(arg_keys[10], (3,), jnp.float32, 0.5, 2.0), 0.5, 2.0)
    return dict(ray_weights=ray_weights, ray_sector=ray_sector, ray_block=ray_block, ray_offset=ray_offset, ray_resid=ray_resid, smooth_resid=smooth_resid, model_dir=model_dir, search_dir=search_dir, model=model, stencil_coeffs=stencil_coeffs, lsqr_scalars=lsqr_scalars)


EPSILON = 1e-06

def smoothing(grid_field, stencil_coeffs):
    along_lon = stencil_coeffs[0]
    along_lat = stencil_coeffs[1]
    along_depth = stencil_coeffs[2]
    damping = stencil_coeffs[3]
    lat_padded = jnp.pad(grid_field, ((0, 0), (1, 1), (0, 0)))
    depth_padded = jnp.pad(grid_field, ((0, 0), (0, 0), (1, 1)))
    diagonal = 2.0 * (along_lon + along_lat + along_depth) + damping
    return diagonal * grid_field - along_lon * (jnp.roll(grid_field, -1, 0) + jnp.roll(grid_field, 1, 0)) - along_lat * (lat_padded[:, 2:] + lat_padded[:, :-2]) - along_depth * (depth_padded[:, :, 2:] + depth_padded[:, :, :-2])

def reference(ray_weights, ray_sector, ray_block, ray_offset, ray_resid, smooth_resid, model_dir, search_dir, model, stencil_coeffs, lsqr_scalars):
    row_ratio = math.sqrt((RAYS + CELLS) / CELLS)
    alpha_now = lsqr_scalars[0]
    rho_bar = lsqr_scalars[1]
    phi_bar = lsqr_scalars[2]
    start = (ray_sector[:, 0] * (LON_DEV * NLAT) + ray_block) * NDEP + ray_offset
    sample_index = start[:, None] + jnp.arange(BAND, dtype=jnp.int32)[None, :]
    flat_dir = model_dir.reshape(-1)
    weights_full = ray_weights.astype(jnp.float32)
    path_sum = lax.optimization_barrier(jnp.sum(weights_full * jnp.take(flat_dir, sample_index), axis=1))
    u_sent = lax.optimization_barrier(ray_resid.astype(jnp.bfloat16)).astype(jnp.float32)
    ray_raw = row_ratio * path_sum - alpha_now * u_sent
    smooth_raw = row_ratio * smoothing(model_dir, stencil_coeffs) - alpha_now * smooth_resid
    beta_total = jnp.sum(ray_raw * ray_raw) + jnp.sum(smooth_raw * smooth_raw)
    beta_now = jnp.sqrt(beta_total / (RAYS + CELLS) + EPSILON)
    ray_new = ray_raw / beta_now
    smooth_new = smooth_raw / beta_now
    scattered = jax.ops.segment_sum((weights_full * ray_new[:, None]).reshape(-1), sample_index.reshape(-1), num_segments=CELLS)
    backward = scattered.reshape(model_dir.shape) + smoothing(smooth_new, stencil_coeffs)
    dir_raw = backward / row_ratio - beta_now * model_dir
    alpha_new = jnp.sqrt(jnp.sum(dir_raw * dir_raw) / CELLS + EPSILON)
    dir_new = dir_raw / alpha_new
    rho_now = jnp.sqrt(rho_bar * rho_bar + beta_now * beta_now)
    cosine = rho_bar / rho_now
    sine = beta_now / rho_now
    theta_now = sine * alpha_new
    rho_bar_new = -cosine * alpha_new
    phi_now = cosine * phi_bar
    phi_bar_new = sine * phi_bar
    model_new = model + phi_now / rho_now * search_dir
    search_new = dir_new - theta_now / rho_now * search_dir
    scalars_new = jnp.stack([alpha_new, beta_now, rho_bar_new, phi_bar_new])
    return (model_new, search_new, dir_new, ray_new, smooth_new, scalars_new)
```

```python
import functools
import math

import jax
import jax.numpy as jnp
from jax import lax
from jax.experimental import pallas as pl
from jax.experimental.pallas import tpu as pltpu
from jax.sharding import PartitionSpec as P

EPSILON = 1e-06
MESH = pl.DeviceIdType.MESH
F32 = jnp.float32
BF16 = jnp.bfloat16
LANES = 128
META = 16
TILE = 16
CHUNK_BLOCKS = 4
NT = (((1,), (1,)), ((), ()))
NN = (((1,), (0,)), ((), ()))


def dot(a, b, dims=NN):
    return lax.dot_general(a, b, dims, preferred_element_type=F32)


def kernel(
    cfg,
    coef_ref,
    rows_ref,
    w_ref,
    v_ref,
    resid_ref,
    sr_ref,
    back_ref,
    home_ref,
    sums_ref,
    msg,
    rays,
    halo,
    psend,
    vhi,
    vlo,
    wx,
    rr,
    ret_send,
    ret_recv,
    a_send,
    a_recv,
    y_send,
    y_recv,
    c_send,
    c_recv,
    d_send,
    d_recv,
    h_send,
    h_recv,
    hy_send,
    hy_recv,
    hc_send,
    hc_recv,
    hd_send,
    hd_recv,
    r_send,
    r_recv,
):
    n, groups, capp, ray_count, lat, depth, ratio = cfg
    me = lax.axis_index("lon")
    g = lax.axis_index("grp")
    gy = lax.rem(g + 2, 4)
    gc = g + 1 - 2 * lax.rem(g, 2)
    right = lax.rem(me + 1, n)
    left = lax.rem(me + n - 1, n)
    share = lat // groups
    q0 = pl.multiple_of(g * share, share)
    qy0 = pl.multiple_of(gy * share, share)
    k0 = coef_ref[0]
    k1 = coef_ref[1]
    k2 = coef_ref[2]
    diag = 2.0 * (k0 + k1 + k2) + coef_ref[3]
    alpha = coef_ref[4]

    barrier = pltpu.get_barrier_semaphore()

    def greet(d, carry):
        pl.semaphore_signal(
            barrier, inc=1, device_id=(lax.rem(me + d, n), g), device_id_type=MESH
        )
        return carry

    lax.fori_loop(1, n, greet, 0)
    pl.semaphore_signal(barrier, inc=1, device_id=(me, gy), device_id_type=MESH)
    pl.semaphore_signal(barrier, inc=1, device_id=(me, gc), device_id_type=MESH)

    target = rows_ref[0:1, :]
    block = rows_ref[1:2, :]
    offset = rows_ref[2:3, :]
    resid = rows_ref[3:4, :]
    sector_rows = -(-n // 16) * 16
    sector_iota = lax.broadcasted_iota(jnp.int32, (sector_rows, ray_count), 0).astype(F32)
    hits = (sector_iota == target).astype(F32)
    before = lax.broadcasted_iota(jnp.int32, (ray_count, ray_count), 0) < lax.broadcasted_iota(
        jnp.int32, (ray_count, ray_count), 1
    )
    rank_all = dot(hits.astype(BF16), jnp.where(before, 1.0, 0.0).astype(BF16))
    slot = target * capp + jnp.sum(hits * rank_all, axis=0, keepdims=True)

    offset_col = jnp.transpose(rows_ref[...])[:, 2:3].astype(jnp.int32)
    turned = w_ref[...].astype(F32)
    for bit in range(7):
        on = lax.rem(offset_col // (1 << bit), 2) == 1
        turned = jnp.where(on, pltpu.roll(turned, 1 << bit, 1), turned)
    turned = turned.astype(BF16)
    block_high = jnp.floor(block * (1.0 / 32))
    offset_high = jnp.floor(offset * (1.0 / 32))
    fields = jnp.concatenate(
        [
            block_high,
            block - 32.0 * block_high,
            offset_high,
            offset - 32.0 * offset_high,
            resid,
            jnp.zeros((META - 5, ray_count), F32),
        ],
        axis=0,
    ).astype(BF16)
    slot_iota = lax.broadcasted_iota(jnp.int32, (capp, ray_count), 0)

    def chosen(s):
        return jnp.where(slot == (slot_iota + s * capp).astype(F32), 1.0, 0.0).astype(BF16)

    def fill(s, carry):
        picked = chosen(s)
        msg[s, :capp, :] = dot(picked, turned).astype(BF16)
        msg[s, capp:, :] = dot(fields, picked, NT).astype(BF16)
        return carry

    lax.fori_loop(0, n, fill, 0)
    rays[g, me] = msg[me]

    pl.semaphore_wait(barrier, n + 1)

    def route(d):
        peer = lax.rem(me + d, n)
        return pltpu.make_async_remote_copy(
            msg.at[peer], rays.at[g, me], a_send.at[d], a_recv.at[d],
            device_id=(peer, g), device_id_type=MESH,
        )

    def route_start(d, carry):
        route(d).start()
        return carry

    lax.fori_loop(1, n, route_start, 0)

    lane = lax.broadcasted_iota(jnp.int32, (TILE, depth), 1)
    first_lane = lane == 0
    last_lane = lane == depth - 1

    def planar(ref, layer, start):
        low = ref[layer, pl.ds(pl.multiple_of(jnp.maximum(start - 8, 0), 8), 8), :]
        low = low * jnp.where(start > 0, 1.0, 0.0)
        high = ref[layer, pl.ds(pl.multiple_of(jnp.minimum(start + TILE, lat - 8), 8), 8), :]
        high = high * jnp.where(start + TILE < lat, 1.0, 0.0)
        mid = ref[layer, pl.ds(start, TILE), :]
        tall = jnp.concatenate([low, mid, high], axis=0)
        rows = TILE + 16
        along_lat = pltpu.roll(tall, 1, 0)[8 : 8 + TILE] + pltpu.roll(tall, rows - 1, 0)[8 : 8 + TILE]
        along_depth = jnp.where(first_lane, 0.0, pltpu.roll(mid, 1, 1)) + jnp.where(
            last_lane, 0.0, pltpu.roll(mid, depth - 1, 1)
        )
        return diag * mid - k1 * along_lat - k2 * along_depth, mid

    for layer in range(2):

        def outer(t, carry, layer=layer):
            start = pl.multiple_of(q0 + t * TILE, TILE)
            plane, _ = planar(v_ref, layer, start)
            other = v_ref[1 - layer, pl.ds(start, TILE), :]
            psend[layer, pl.ds(pl.multiple_of(t * TILE, TILE), TILE), :] = (
                ratio * (plane - k0 * other) - alpha * resid_ref[layer, pl.ds(start, TILE), :]
            )
            return carry

        lax.fori_loop(0, share // TILE, outer, 0)

    own = pl.ds(q0, share)
    sources = [
        (v_ref.at[1, own], right),
        (v_ref.at[0, own], left),
        (psend.at[1], right),
        (psend.at[0], left),
    ]
    halo_copies = [
        pltpu.make_async_remote_copy(
            src, halo.at[i, own], h_send.at[i], h_recv.at[i],
            device_id=(peer, g), device_id_type=MESH,
        )
        for i, (src, peer) in enumerate(sources)
    ]
    for copy in halo_copies:
        copy.start()

    def split(t, carry):
        rows = pl.ds(pl.multiple_of(t * TILE, TILE), TILE)
        for layer in range(2):
            x = v_ref[layer, rows, :]
            high = x.astype(BF16)
            target_rows = pl.ds(pl.multiple_of(layer * lat + t * TILE, TILE), TILE)
            vhi[target_rows, :] = high
            vlo[target_rows, :] = (x - high.astype(F32)).astype(BF16)
            back_ref[layer, rows, :] = jnp.zeros((TILE, depth), F32)
        return carry

    lax.fori_loop(0, lat // TILE, split, 0)

    def along_y(d):
        src = rays.at[g, lax.rem(me - d + n, n)]
        return pltpu.make_async_remote_copy(
            src, src, y_send.at[d], y_recv.at[d], device_id=(me, gy), device_id_type=MESH
        )

    def along_c(d):
        src = rays.at[g, lax.rem(me - d + n, n)]
        return pltpu.make_async_remote_copy(
            src, src, c_send.at[d], c_recv.at[d], device_id=(me, gc), device_id_type=MESH
        )

    def along_d(d):
        src = rays.at[gy, lax.rem(me - d + n, n)]
        return pltpu.make_async_remote_copy(
            src, src, d_send.at[d], d_recv.at[d], device_id=(me, gc), device_id_type=MESH
        )

    along_y(0).start()
    along_c(0).start()

    def pass_on(d, carry):
        route(d).wait_recv()
        along_y(d).start()
        along_c(d).start()
        return carry

    lax.fori_loop(1, n, pass_on, 0)

    def pass_again(d, carry):
        along_y(d).wait_recv()
        along_d(d).start()
        return carry

    lax.fori_loop(0, n, pass_again, 0)

    hy = []
    hc = []
    for i in range(4):
        halo_copies[i].wait_recv()
        piece = halo.at[i, own]
        hy.append(
            pltpu.make_async_remote_copy(
                piece, piece, hy_send.at[i], hy_recv.at[i],
                device_id=(me, gy), device_id_type=MESH,
            )
        )
        hc.append(
            pltpu.make_async_remote_copy(
                piece, piece, hc_send.at[i], hc_recv.at[i],
                device_id=(me, gc), device_id_type=MESH,
            )
        )
        hy[i].start()
        hc[i].start()

    def settle(d, carry):
        along_c(d).wait_recv()
        along_d(d).wait_recv()
        return carry

    lax.fori_loop(0, n, settle, 0)

    per_group = n // CHUNK_BLOCKS
    chunk = CHUNK_BLOCKS * capp
    cells = 2 * lat
    cell_tile = math.gcd(cells, 256)
    cell_iota = lax.broadcasted_iota(jnp.int32, (cell_tile, chunk), 0)
    spot = lax.broadcasted_iota(jnp.int32, (capp, LANES), 1)

    def ray_chunk(c, square):
        source_group = c // per_group
        base = lax.rem(c, per_group) * CHUNK_BLOCKS
        block_rows = []
        resid_rows = []
        for i in range(CHUNK_BLOCKS):
            meta = rays[source_group, base + i, capp:, :].astype(F32)
            block_rows.append(meta[0:1] * 32.0 + meta[1:2])
            resid_rows.append(meta[4:5])
            start = jnp.broadcast_to(meta[2:3] * 32.0 + meta[3:4], (8, capp))
            start_col = jnp.transpose(start)[:, 0:1].astype(jnp.int32)
            weights = rays[source_group, base + i, :capp, :].astype(F32)
            for j in range(depth // LANES):
                where = spot + (j * LANES) - start_col
                inside = (where >= 0) & (where < LANES)
                wx[i * capp : (i + 1) * capp, j * LANES : (j + 1) * LANES] = jnp.where(
                    inside, weights, 0.0
                ).astype(BF16)
        block_row = jnp.concatenate(block_rows, axis=1).astype(jnp.int32)
        resid_row = jnp.concatenate(resid_rows, axis=1)

        def product(t, total):
            rows = pl.ds(pl.multiple_of(t * cell_tile, cell_tile), cell_tile)
            found = dot(vhi[rows, :], wx[...], NT) + dot(vlo[rows, :], wx[...], NT)
            hit = (cell_iota + t * cell_tile) == block_row
            return total + jnp.sum(jnp.where(hit, found, 0.0), axis=0, keepdims=True)

        path = lax.fori_loop(0, cells // cell_tile, product, jnp.zeros((1, chunk), F32))
        raw = ratio * path - alpha * resid_row
        for i in range(CHUNK_BLOCKS):
            rr[source_group * n + base + i] = jnp.broadcast_to(
                raw[:, i * capp : (i + 1) * capp], (8, capp)
            )
        raw_high = raw.astype(BF16).astype(F32)
        raw_low = raw - raw_high

        def spread(t, carry):
            layer = t * cell_tile // lat
            rows = pl.ds(pl.multiple_of(lax.rem(t * cell_tile, lat), cell_tile), cell_tile)
            hit = (cell_iota + t * cell_tile) == block_row
            back_ref[layer, rows, :] += dot(
                jnp.where(hit, raw_high, 0.0).astype(BF16), wx[...]
            ) + dot(jnp.where(hit, raw_low, 0.0).astype(BF16), wx[...])
            return carry

        lax.fori_loop(0, cells // cell_tile, spread, 0)
        return square + raw * raw

    chunks = groups * per_group
    square = lax.fori_loop(0, chunks // 2, ray_chunk, jnp.zeros((1, chunk), F32))
    hd = []
    for i in range(4):
        hy[i].wait_recv()
        piece = halo.at[i, pl.ds(qy0, share)]
        hd.append(
            pltpu.make_async_remote_copy(
                piece, piece, hd_send.at[i], hd_recv.at[i],
                device_id=(me, gc), device_id_type=MESH,
            )
        )
        hd[i].start()
    square = lax.fori_loop(chunks // 2, chunks, ray_chunk, square)
    ray_square = jnp.sum(square)
    for i in range(4):
        hc[i].wait_recv()
        hd[i].wait_recv()

    def fold(x):
        return jnp.sum(x.reshape(TILE // 8, 8, depth), axis=0)

    zero = jnp.zeros((8, depth), F32)
    smooth_square = zero
    for layer in range(2):

        def forward(t, total, layer=layer):
            start = pl.multiple_of(t * TILE, TILE)
            rows = pl.ds(start, TILE)
            plane, _ = planar(v_ref, layer, start)
            beside = halo[layer, rows, :] + v_ref[1 - layer, rows, :]
            raw = ratio * (plane - k0 * beside) - alpha * resid_ref[layer, rows, :]
            sr_ref[layer, rows, :] = raw
            return total + fold(raw * raw)

        smooth_square = lax.fori_loop(0, lat // TILE, forward, smooth_square)

    totals = (zero, zero, zero)
    for layer in range(2):

        def transposed(t, totals, layer=layer):
            start = pl.multiple_of(t * TILE, TILE)
            rows = pl.ds(start, TILE)
            plane, _ = planar(sr_ref, layer, start)
            x = v_ref[layer, rows, :]
            outside = halo[2 + layer, rows, :] - (ratio * k0) * x
            value = back_ref[layer, rows, :] + plane - k0 * (outside + sr_ref[1 - layer, rows, :])
            back_ref[layer, rows, :] = value
            return (
                totals[0] + fold(value * value),
                totals[1] + fold(value * x),
                totals[2] + fold(x * x),
            )

        totals = lax.fori_loop(0, lat // TILE, transposed, totals)

    sub = lax.broadcasted_iota(jnp.int32, (8, LANES), 0)
    col = lax.broadcasted_iota(jnp.int32, (8, LANES), 1)
    numbers = [ray_square + jnp.sum(smooth_square)] + [jnp.sum(x) for x in totals]
    sums = jnp.zeros((8, LANES), F32)
    for i, number in enumerate(numbers):
        sums = jnp.where(col == i, number, sums)

    def answer(s, carry):
        ret_send[s] = jnp.where(sub == 0, rr[g * n + s], sums)
        return carry

    lax.fori_loop(0, n, answer, 0)
    ret_recv[me] = ret_send[me]

    def give_back(d):
        peer = lax.rem(me + d, n)
        return pltpu.make_async_remote_copy(
            ret_send.at[peer], ret_recv.at[me], r_send.at[d], r_recv.at[d],
            device_id=(peer, g), device_id_type=MESH,
        )

    def give_start(d, carry):
        give_back(d).start()
        return carry

    def give_wait(d, carry):
        give_back(d).wait_recv()
        return carry

    lax.fori_loop(1, n, give_start, 0)
    lax.fori_loop(1, n, give_wait, 0)

    def collect(s, carry):
        total, home = carry
        tile = ret_recv[s]
        one = tile.astype(BF16).astype(F32)
        two = (tile - one).astype(BF16).astype(F32)
        three = tile - one - two
        stack = jnp.concatenate([one, two, three, jnp.zeros((8, LANES), F32)], axis=0).astype(BF16)
        got = dot(stack, chosen(s))
        return total + tile, home + (got[0:8] + got[8:16] + got[16:24])

    total, home = lax.fori_loop(
        0, n, collect, (jnp.zeros((8, LANES), F32), jnp.zeros((8, ray_count), F32))
    )
    sums_ref[...] = total
    home_ref[...] = home

    def finish(d, carry):
        route(d).wait_send()
        give_back(d).wait_send()
        return carry

    lax.fori_loop(1, n, finish, 0)

    def finish_all(d, carry):
        along_y(d).wait_send()
        along_c(d).wait_send()
        along_d(d).wait_send()
        return carry

    lax.fori_loop(0, n, finish_all, 0)
    for copy in halo_copies + hy + hc + hd:
        copy.wait_send()


def on_device(
    ray_weights,
    ray_sector,
    ray_block,
    ray_offset,
    ray_resid,
    smooth_resid,
    model_dir,
    search_dir,
    model,
    stencil_coeffs,
    lsqr_scalars,
):
    n = lax.axis_size("lon")
    groups = lax.axis_size("grp")
    ray_count = ray_weights.shape[0]
    lon_cells, lat, depth = model_dir.shape
    assert lon_cells == 2 and groups == 4 and n % CHUNK_BLOCKS == 0
    capacity = 2 * ray_count // n
    capp = -(-capacity // LANES) * LANES
    assert capp == LANES
    cells_total = lon_cells * lat * depth * n
    rows_total = ray_count * n * groups + cells_total
    ratio = math.sqrt(rows_total / cells_total)
    rows = jnp.concatenate(
        [
            jnp.stack(
                [
                    ray_sector[:, 0].astype(F32),
                    ray_block.astype(F32),
                    ray_offset.astype(F32),
                    ray_resid.astype(BF16).astype(F32),
                ]
            ),
            jnp.zeros((4, ray_count), F32),
        ]
    )
    coef = jnp.concatenate([stencil_coeffs, lsqr_scalars])
    field = jax.ShapeDtypeStruct((2, lat, depth), F32)
    vmem = pl.BlockSpec(memory_space=pltpu.VMEM)
    dma = pltpu.SemaphoreType.DMA
    cfg = (n, groups, capp, ray_count, lat, depth, ratio)
    smooth_raw, back, home, sums = pl.pallas_call(
        functools.partial(kernel, cfg),
        out_shape=(
            field,
            field,
            jax.ShapeDtypeStruct((8, ray_count), F32),
            jax.ShapeDtypeStruct((8, LANES), F32),
        ),
        in_specs=[pl.BlockSpec(memory_space=pltpu.SMEM)] + [vmem] * 4,
        out_specs=(vmem,) * 4,
        scratch_shapes=[
            pltpu.VMEM((n, capp + META, LANES), BF16),
            pltpu.VMEM((groups, n, capp + META, LANES), BF16),
            pltpu.VMEM((4, lat, depth), F32),
            pltpu.VMEM((2, lat // groups, depth), F32),
            pltpu.VMEM((2 * lat, depth), BF16),
            pltpu.VMEM((2 * lat, depth), BF16),
            pltpu.VMEM((CHUNK_BLOCKS * capp, depth), BF16),
            pltpu.VMEM((groups * n, 8, capp), F32),
            pltpu.VMEM((n, 8, LANES), F32),
            pltpu.VMEM((n, 8, LANES), F32),
        ]
        + [dma((n,))] * 8
        + [dma((4,))] * 8
        + [dma((n,))] * 2,
        compiler_params=pltpu.CompilerParams(
            collective_id=0, has_side_effects=True, vmem_limit_bytes=48 * 1024 * 1024
        ),
        cost_estimate=pl.CostEstimate(
            flops=20_000_000_000, bytes_accessed=8_000_000, transcendentals=0
        ),
    )(coef, rows, ray_weights, model_dir, smooth_resid)

    alpha_now = lsqr_scalars[0]
    rho_bar = lsqr_scalars[1]
    phi_bar = lsqr_scalars[2]
    beta_now = jnp.sqrt(sums[1, 0] / rows_total + EPSILON)
    scale = 1.0 / (beta_now * ratio)
    alpha_total = (
        scale * scale * sums[1, 1]
        - 2.0 * (scale * beta_now) * sums[1, 2]
        + beta_now * beta_now * sums[1, 3]
    )
    alpha_new = jnp.sqrt(jnp.maximum(alpha_total, 0.0) / cells_total + EPSILON)
    rho_now = jnp.sqrt(rho_bar * rho_bar + beta_now * beta_now)
    cosine = rho_bar / rho_now
    sine = beta_now / rho_now
    theta_now = sine * alpha_new
    rho_bar_new = -cosine * alpha_new
    phi_now = cosine * phi_bar
    phi_bar_new = sine * phi_bar
    beta_inverse = 1.0 / beta_now
    dir_new = back * (scale / alpha_new) - model_dir * (beta_now / alpha_new)
    smooth_new = smooth_raw * beta_inverse
    ray_resid_new = home[0] * beta_inverse
    model_new = model + phi_now / rho_now * search_dir
    search_new = dir_new - theta_now / rho_now * search_dir
    scalars_new = jnp.stack([alpha_new, beta_now, rho_bar_new, phi_bar_new])
    return (model_new, search_new, dir_new, ray_resid_new, smooth_new, scalars_new)


def solution(mesh):
    placed = (
        P(("lon", "grp"), None),
        P(("lon", "grp"), None),
        P(("lon", "grp")),
        P(("lon", "grp")),
        P(("lon", "grp")),
        P("lon", None, None),
        P("lon", None, None),
        P("lon", None, None),
        P("lon", None, None),
        P(),
        P(),
    )
    return jax.shard_map(
        on_device,
        mesh=mesh,
        in_specs=placed,
        out_specs=(
            P("lon", None, None),
            P("lon", None, None),
            P("lon", None, None),
            P(("lon", "grp")),
            P("lon", None, None),
            P(),
        ),
        check_vma=False,
    )
```

```python
import functools
import math

import jax
import jax.numpy as jnp
from jax import lax
from jax.experimental import pallas as pl
from jax.experimental.pallas import tpu as pltpu
from jax.sharding import PartitionSpec as P

EPSILON = 1e-06
MESH = pl.DeviceIdType.MESH
F32 = jnp.float32
BF16 = jnp.bfloat16
LANES = 128
META = 16
TILE = 16
CHUNK_BLOCKS = 4
NT = (((1,), (1,)), ((), ()))
NN = (((1,), (0,)), ((), ()))


def dot(a, b, dims=NN):
    return lax.dot_general(a, b, dims, preferred_element_type=F32)


def kernel(
    cfg,
    stencil_ref,
    scalar_ref,
    sector_ref,
    block_ref,
    offset_ref,
    left_ref,
    w_ref,
    v_ref,
    resid_ref,
    sr_ref,
    back_ref,
    home_ref,
    coef_ref,
    msg,
    rays,
    halo,
    psend,
    vhi,
    vlo,
    wx,
    rr,
    ret_send,
    ret_recv,
    a_send,
    a_recv,
    y_send,
    y_recv,
    c_send,
    c_recv,
    d_send,
    d_recv,
    h_send,
    h_recv,
    hy_send,
    hy_recv,
    hc_send,
    hc_recv,
    hd_send,
    hd_recv,
    r_send,
    r_recv,
):
    n, groups, capp, ray_count, lat, depth, ratio, rows_total, cells_total = cfg
    me = lax.axis_index("lon")
    g = lax.axis_index("grp")
    gy = lax.rem(g + 2, 4)
    gc = g + 1 - 2 * lax.rem(g, 2)
    right = lax.rem(me + 1, n)
    left = lax.rem(me + n - 1, n)
    share = lat // groups
    q0 = pl.multiple_of(g * share, share)
    qy0 = pl.multiple_of(gy * share, share)
    k0 = stencil_ref[0]
    k1 = stencil_ref[1]
    k2 = stencil_ref[2]
    diag = 2.0 * (k0 + k1 + k2) + stencil_ref[3]
    alpha = scalar_ref[0]

    barrier = pltpu.get_barrier_semaphore()

    def greet(d, carry):
        pl.semaphore_signal(
            barrier, inc=1, device_id=(lax.rem(me + d, n), g), device_id_type=MESH
        )
        return carry

    lax.fori_loop(1, n, greet, 0)
    pl.semaphore_signal(barrier, inc=1, device_id=(me, gy), device_id_type=MESH)
    pl.semaphore_signal(barrier, inc=1, device_id=(me, gc), device_id_type=MESH)

    pl.semaphore_wait(barrier, n + 1)

    own = pl.ds(q0, share)
    sources = [
        (v_ref.at[1, own], right),
        (v_ref.at[0, own], left),
        (psend.at[1], right),
        (psend.at[0], left),
    ]
    halo_copies = [
        pltpu.make_async_remote_copy(
            src, halo.at[i, own], h_send.at[i], h_recv.at[i],
            device_id=(peer, g), device_id_type=MESH,
        )
        for i, (src, peer) in enumerate(sources)
    ]
    for copy in halo_copies[:2]:
        copy.start()

    target = sector_ref[...].astype(F32)
    block = block_ref[...].astype(F32)
    offset = offset_ref[...].astype(F32)
    resid = left_ref[...]
    sector_rows = -(-n // 16) * 16
    sector_iota = lax.broadcasted_iota(jnp.int32, (sector_rows, ray_count), 0).astype(F32)
    hits = (sector_iota == target).astype(F32)
    before = lax.broadcasted_iota(jnp.int32, (ray_count, ray_count), 0) < lax.broadcasted_iota(
        jnp.int32, (ray_count, ray_count), 1
    )
    rank_all = dot(hits.astype(BF16), jnp.where(before, 1.0, 0.0).astype(BF16))
    slot = target * capp + jnp.sum(hits * rank_all, axis=0, keepdims=True)

    offset_col = jnp.transpose(jnp.broadcast_to(offset, (8, ray_count)))[:, 0:1].astype(jnp.int32)
    turned = w_ref[...].astype(F32)
    for bit in range(7):
        on = lax.rem(offset_col // (1 << bit), 2) == 1
        turned = jnp.where(on, pltpu.roll(turned, 1 << bit, 1), turned)
    turned = turned.astype(BF16)
    block_high = jnp.floor(block * (1.0 / 32))
    offset_high = jnp.floor(offset * (1.0 / 32))
    fields = jnp.concatenate(
        [
            block_high,
            block - 32.0 * block_high,
            offset_high,
            offset - 32.0 * offset_high,
            resid,
            jnp.zeros((META - 5, ray_count), F32),
        ],
        axis=0,
    ).astype(BF16)
    slot_iota = lax.broadcasted_iota(jnp.int32, (capp, ray_count), 0)

    def chosen(s):
        return jnp.where(slot == (slot_iota + s * capp).astype(F32), 1.0, 0.0).astype(BF16)

    def fill(s, carry):
        picked = chosen(s)
        msg[s, :capp, :] = dot(picked, turned).astype(BF16)
        msg[s, capp:, :] = dot(fields, picked, NT).astype(BF16)
        return carry

    lax.fori_loop(0, n, fill, 0)
    rays[g, me] = msg[me]

    def route(d):
        peer = lax.rem(me + d, n)
        return pltpu.make_async_remote_copy(
            msg.at[peer], rays.at[g, me], a_send.at[d], a_recv.at[d],
            device_id=(peer, g), device_id_type=MESH,
        )

    def route_start(d, carry):
        route(d).start()
        return carry

    lax.fori_loop(1, n, route_start, 0)

    lane = lax.broadcasted_iota(jnp.int32, (TILE, depth), 1)
    first_lane = lane == 0
    last_lane = lane == depth - 1

    def planar(ref, layer, start):
        low = ref[layer, pl.ds(pl.multiple_of(jnp.maximum(start - 8, 0), 8), 8), :]
        low = low * jnp.where(start > 0, 1.0, 0.0)
        high = ref[layer, pl.ds(pl.multiple_of(jnp.minimum(start + TILE, lat - 8), 8), 8), :]
        high = high * jnp.where(start + TILE < lat, 1.0, 0.0)
        mid = ref[layer, pl.ds(start, TILE), :]
        tall = jnp.concatenate([low, mid, high], axis=0)
        rows = TILE + 16
        along_lat = pltpu.roll(tall, 1, 0)[8 : 8 + TILE] + pltpu.roll(tall, rows - 1, 0)[8 : 8 + TILE]
        along_depth = jnp.where(first_lane, 0.0, pltpu.roll(mid, 1, 1)) + jnp.where(
            last_lane, 0.0, pltpu.roll(mid, depth - 1, 1)
        )
        return diag * mid - k1 * along_lat - k2 * along_depth, mid

    for layer in range(2):

        def outer(t, carry, layer=layer):
            start = pl.multiple_of(q0 + t * TILE, TILE)
            plane, _ = planar(v_ref, layer, start)
            other = v_ref[1 - layer, pl.ds(start, TILE), :]
            psend[layer, pl.ds(pl.multiple_of(t * TILE, TILE), TILE), :] = (
                ratio * (plane - k0 * other) - alpha * resid_ref[layer, pl.ds(start, TILE), :]
            )
            return carry

        lax.fori_loop(0, share // TILE, outer, 0)

    for copy in halo_copies[2:]:
        copy.start()

    def along_y(d):
        src = rays.at[g, lax.rem(me - d + n, n)]
        return pltpu.make_async_remote_copy(
            src, src, y_send.at[d], y_recv.at[d], device_id=(me, gy), device_id_type=MESH
        )

    def along_c(d):
        src = rays.at[g, lax.rem(me - d + n, n)]
        return pltpu.make_async_remote_copy(
            src, src, c_send.at[d], c_recv.at[d], device_id=(me, gc), device_id_type=MESH
        )

    def along_d(d):
        src = rays.at[gy, lax.rem(me - d + n, n)]
        return pltpu.make_async_remote_copy(
            src, src, d_send.at[d], d_recv.at[d], device_id=(me, gc), device_id_type=MESH
        )

    along_y(0).start()
    along_c(0).start()

    def pass_on(d, carry):
        route(d).wait_recv()
        along_y(d).start()
        along_c(d).start()
        return carry

    lax.fori_loop(1, n, pass_on, 0)

    def split(t, carry):
        rows = pl.ds(pl.multiple_of(t * TILE, TILE), TILE)
        for layer in range(2):
            x = v_ref[layer, rows, :]
            high = x.astype(BF16)
            target_rows = pl.ds(pl.multiple_of(layer * lat + t * TILE, TILE), TILE)
            vhi[target_rows, :] = high
            vlo[target_rows, :] = (x - high.astype(F32)).astype(BF16)
            back_ref[layer, rows, :] = jnp.zeros((TILE, depth), F32)
        return carry

    lax.fori_loop(0, lat // TILE, split, 0)

    for layer in range(2):

        def inner(t, carry, layer=layer):
            start = pl.multiple_of(t * TILE, TILE)
            rows = pl.ds(start, TILE)
            plane, _ = planar(v_ref, layer, start)
            sr_ref[layer, rows, :] = (
                ratio * (plane - k0 * v_ref[1 - layer, rows, :])
                - alpha * resid_ref[layer, rows, :]
            )
            return carry

        lax.fori_loop(0, lat // TILE, inner, 0)

    def pass_again(d, carry):
        along_y(d).wait_recv()
        along_d(d).start()
        return carry

    lax.fori_loop(0, n, pass_again, 0)

    def piece_to(rows, sends, recvs, to):
        return [
            pltpu.make_async_remote_copy(
                halo.at[i, rows], halo.at[i, rows], sends.at[i], recvs.at[i],
                device_id=(me, to), device_id_type=MESH,
            )
            for i in range(4)
        ]

    hy = piece_to(own, hy_send, hy_recv, gy)
    hc = piece_to(own, hc_send, hc_recv, gc)
    hd = piece_to(pl.ds(qy0, share), hd_send, hd_recv, gc)

    def halo_on(first):
        for i in (first, first + 1):
            halo_copies[i].wait_recv()
            hy[i].start()
            hc[i].start()

    def halo_again(first):
        for i in (first, first + 1):
            hy[i].wait_recv()
            hd[i].start()

    halo_on(0)

    def settle(d, carry):
        along_c(d).wait_recv()
        along_d(d).wait_recv()
        return carry

    lax.fori_loop(0, n, settle, 0)

    per_group = n // CHUNK_BLOCKS
    chunk = CHUNK_BLOCKS * capp
    cells = 2 * lat
    cell_tile = math.gcd(cells, 256)
    cell_iota = lax.broadcasted_iota(jnp.int32, (cell_tile, chunk), 0)
    spot = lax.broadcasted_iota(jnp.int32, (capp, LANES), 1)

    def ray_chunk(c, square):
        source_group = c // per_group
        base = lax.rem(c, per_group) * CHUNK_BLOCKS
        block_rows = []
        resid_rows = []
        for i in range(CHUNK_BLOCKS):
            meta = rays[source_group, base + i, capp:, :].astype(F32)
            block_rows.append(meta[0:1] * 32.0 + meta[1:2])
            resid_rows.append(meta[4:5])
            start = jnp.broadcast_to(meta[2:3] * 32.0 + meta[3:4], (8, capp))
            start_col = jnp.transpose(start)[:, 0:1].astype(jnp.int32)
            weights = rays[source_group, base + i, :capp, :].astype(F32)
            for j in range(depth // LANES):
                where = spot + (j * LANES) - start_col
                inside = (where >= 0) & (where < LANES)
                wx[i * capp : (i + 1) * capp, j * LANES : (j + 1) * LANES] = jnp.where(
                    inside, weights, 0.0
                ).astype(BF16)
        block_row = jnp.concatenate(block_rows, axis=1).astype(jnp.int32)
        resid_row = jnp.concatenate(resid_rows, axis=1)

        def product(t, total):
            rows = pl.ds(pl.multiple_of(t * cell_tile, cell_tile), cell_tile)
            found = dot(vhi[rows, :], wx[...], NT) + dot(vlo[rows, :], wx[...], NT)
            hit = (cell_iota + t * cell_tile) == block_row
            return total + jnp.sum(jnp.where(hit, found, 0.0), axis=0, keepdims=True)

        path = lax.fori_loop(0, cells // cell_tile, product, jnp.zeros((1, chunk), F32))
        raw = ratio * path - alpha * resid_row
        for i in range(CHUNK_BLOCKS):
            rr[source_group * n + base + i] = jnp.broadcast_to(
                raw[:, i * capp : (i + 1) * capp], (8, capp)
            )
        raw_high = raw.astype(BF16).astype(F32)
        raw_low = raw - raw_high

        def spread(t, carry):
            layer = t * cell_tile // lat
            rows = pl.ds(pl.multiple_of(lax.rem(t * cell_tile, lat), cell_tile), cell_tile)
            hit = (cell_iota + t * cell_tile) == block_row
            back_ref[layer, rows, :] += dot(
                jnp.where(hit, raw_high, 0.0).astype(BF16), wx[...]
            ) + dot(jnp.where(hit, raw_low, 0.0).astype(BF16), wx[...])
            return carry

        lax.fori_loop(0, cells // cell_tile, spread, 0)
        return square + raw * raw

    chunks = groups * per_group
    square = jnp.zeros((1, chunk), F32)
    bounds = [chunks * i // 8 for i in (0, 1, 4, 7, 8)]
    for i, step in enumerate((lambda: halo_on(2), lambda: halo_again(0), lambda: halo_again(2), None)):
        square = lax.fori_loop(bounds[i], bounds[i + 1], ray_chunk, square)
        if step is not None:
            step()
    ray_square = jnp.sum(square)
    for i in range(4):
        hc[i].wait_recv()
        hd[i].wait_recv()

    def fold(x):
        return jnp.sum(x.reshape(TILE // 8, 8, depth), axis=0)

    zero = jnp.zeros((8, depth), F32)
    smooth_square = zero
    for layer in range(2):

        def forward(t, total, layer=layer):
            start = pl.multiple_of(t * TILE, TILE)
            rows = pl.ds(start, TILE)
            raw = sr_ref[layer, rows, :] - (ratio * k0) * halo[layer, rows, :]
            sr_ref[layer, rows, :] = raw
            return total + fold(raw * raw)

        smooth_square = lax.fori_loop(0, lat // TILE, forward, smooth_square)

    totals = (zero, zero, zero)
    for layer in range(2):

        def transposed(t, totals, layer=layer):
            start = pl.multiple_of(t * TILE, TILE)
            rows = pl.ds(start, TILE)
            plane, _ = planar(sr_ref, layer, start)
            x = v_ref[layer, rows, :]
            outside = halo[2 + layer, rows, :] - (ratio * k0) * x
            value = back_ref[layer, rows, :] + plane - k0 * (outside + sr_ref[1 - layer, rows, :])
            back_ref[layer, rows, :] = value
            return (
                totals[0] + fold(value * value),
                totals[1] + fold(value * x),
                totals[2] + fold(x * x),
            )

        totals = lax.fori_loop(0, lat // TILE, transposed, totals)

    sub = lax.broadcasted_iota(jnp.int32, (8, LANES), 0)
    col = lax.broadcasted_iota(jnp.int32, (8, LANES), 1)
    numbers = [ray_square + jnp.sum(smooth_square)] + [jnp.sum(x) for x in totals]
    sums = jnp.zeros((8, LANES), F32)
    for i, number in enumerate(numbers):
        sums = jnp.where(col == i, number, sums)

    def answer(s, carry):
        ret_send[s] = jnp.where(sub == 0, rr[g * n + s], sums)
        return carry

    lax.fori_loop(0, n, answer, 0)
    ret_recv[me] = ret_send[me]

    def give_back(d):
        peer = lax.rem(me + d, n)
        return pltpu.make_async_remote_copy(
            ret_send.at[peer], ret_recv.at[me], r_send.at[d], r_recv.at[d],
            device_id=(peer, g), device_id_type=MESH,
        )

    def give_start(d, carry):
        give_back(d).start()
        return carry

    def give_wait(d, carry):
        give_back(d).wait_recv()
        return carry

    lax.fori_loop(1, n, give_start, 0)
    lax.fori_loop(1, n, give_wait, 0)

    def collect(s, carry):
        total, home = carry
        tile = ret_recv[s]
        one = tile.astype(BF16).astype(F32)
        two = (tile - one).astype(BF16).astype(F32)
        three = tile - one - two
        stack = jnp.concatenate([one, two, three, jnp.zeros((8, LANES), F32)], axis=0).astype(BF16)
        got = dot(stack, chosen(s))
        return total + tile, home + (got[0:8] + got[8:16] + got[16:24])

    total, home = lax.fori_loop(
        0, n, collect, (jnp.zeros((8, LANES), F32), jnp.zeros((8, ray_count), F32))
    )

    def number_of(i):
        return jnp.broadcast_to(total[1:2, i : i + 1], (8, LANES))

    rho_bar = scalar_ref[1]
    phi_bar = scalar_ref[2]
    beta = jnp.sqrt(number_of(0) / rows_total + EPSILON)
    scale = 1.0 / (beta * ratio)
    spread_sum = (
        scale * scale * number_of(1)
        - 2.0 * (scale * beta) * number_of(2)
        + beta * beta * number_of(3)
    )
    alpha_new = jnp.sqrt(jnp.maximum(spread_sum, 0.0) / cells_total + EPSILON)
    rho = jnp.sqrt(rho_bar * rho_bar + beta * beta)
    cosine = rho_bar / rho
    sine = beta / rho
    results = [
        alpha_new,
        beta,
        -cosine * alpha_new,
        sine * phi_bar,
        cosine * phi_bar / rho,
        sine * alpha_new / rho,
        scale / alpha_new,
        beta / alpha_new,
        1.0 / beta,
    ]
    tile = jnp.zeros((8, LANES), F32)
    for i, result in enumerate(results):
        tile = jnp.where(col == i, result, tile)
    coef_ref[...] = tile
    home_ref[...] = home / beta[:, 0:1]

    def finish(d, carry):
        route(d).wait_send()
        give_back(d).wait_send()
        return carry

    lax.fori_loop(1, n, finish, 0)

    def finish_all(d, carry):
        along_y(d).wait_send()
        along_c(d).wait_send()
        along_d(d).wait_send()
        return carry

    lax.fori_loop(0, n, finish_all, 0)
    for copy in halo_copies + hy + hc + hd:
        copy.wait_send()


def update(coef, raw, back, v, search, model, model_new, search_new, dir_new, smooth_new):
    def value(i):
        return coef[0:1, i : i + 1]

    for layer in range(2):
        turned = back[layer] * value(6) - v[layer] * value(7)
        dir_new[layer] = turned
        search_new[layer] = turned - value(5) * search[layer]
        model_new[layer] = model[layer] + value(4) * search[layer]
        smooth_new[layer] = raw[layer] * value(8)


def on_device(
    ray_weights,
    ray_sector,
    ray_block,
    ray_offset,
    ray_resid,
    smooth_resid,
    model_dir,
    search_dir,
    model,
    stencil_coeffs,
    lsqr_scalars,
):
    n = lax.axis_size("lon")
    groups = lax.axis_size("grp")
    ray_count = ray_weights.shape[0]
    lon_cells, lat, depth = model_dir.shape
    assert lon_cells == 2 and groups == 4 and n % CHUNK_BLOCKS == 0
    capacity = 2 * ray_count // n
    capp = -(-capacity // LANES) * LANES
    assert capp == LANES
    cells_total = lon_cells * lat * depth * n
    rows_total = ray_count * n * groups + cells_total
    ratio = math.sqrt(rows_total / cells_total)
    field = jax.ShapeDtypeStruct((2, lat, depth), F32)
    vmem = pl.BlockSpec(memory_space=pltpu.VMEM)
    dma = pltpu.SemaphoreType.DMA
    cfg = (n, groups, capp, ray_count, lat, depth, ratio, rows_total, cells_total)
    smooth_raw, back, home, coef = pl.pallas_call(
        functools.partial(kernel, cfg),
        out_shape=(
            field,
            field,
            jax.ShapeDtypeStruct((8, ray_count), F32),
            jax.ShapeDtypeStruct((8, LANES), F32),
        ),
        in_specs=[pl.BlockSpec(memory_space=pltpu.SMEM)] * 2 + [vmem] * 7,
        out_specs=(vmem,) * 4,
        scratch_shapes=[
            pltpu.VMEM((n, capp + META, LANES), BF16),
            pltpu.VMEM((groups, n, capp + META, LANES), BF16),
            pltpu.VMEM((4, lat, depth), F32),
            pltpu.VMEM((2, lat // groups, depth), F32),
            pltpu.VMEM((2 * lat, depth), BF16),
            pltpu.VMEM((2 * lat, depth), BF16),
            pltpu.VMEM((CHUNK_BLOCKS * capp, depth), BF16),
            pltpu.VMEM((groups * n, 8, capp), F32),
            pltpu.VMEM((n, 8, LANES), F32),
            pltpu.VMEM((n, 8, LANES), F32),
        ]
        + [dma((n,))] * 8
        + [dma((4,))] * 8
        + [dma((n,))] * 2,
        compiler_params=pltpu.CompilerParams(
            collective_id=0, has_side_effects=True, vmem_limit_bytes=48 * 1024 * 1024
        ),
        cost_estimate=pl.CostEstimate(
            flops=20_000_000_000, bytes_accessed=8_000_000, transcendentals=0
        ),
    )(
        stencil_coeffs,
        lsqr_scalars,
        ray_sector.reshape(1, ray_count),
        ray_block.reshape(1, ray_count),
        ray_offset.reshape(1, ray_count),
        ray_resid.reshape(1, ray_count),
        ray_weights,
        model_dir,
        smooth_resid,
    )

    lat_block = math.gcd(lat, 64)
    whole = pl.BlockSpec((8, LANES), lambda t: (0, 0))
    part = pl.BlockSpec((2, lat_block, depth), lambda t: (0, t, 0))
    model_new, search_new, dir_new, smooth_new = pl.pallas_call(
        update,
        grid=(lat // lat_block,),
        out_shape=(field,) * 4,
        in_specs=[whole] + [part] * 5,
        out_specs=(part,) * 4,
        compiler_params=pltpu.CompilerParams(vmem_limit_bytes=24 * 1024 * 1024),
        cost_estimate=pl.CostEstimate(
            flops=10_000_000, bytes_accessed=18_874_368, transcendentals=0
        ),
    )(coef, smooth_raw, back, model_dir, search_dir, model)
    return (model_new, search_new, dir_new, home[0], smooth_new, coef[0, :4])


def solution(mesh):
    placed = (
        P(("lon", "grp"), None),
        P(("lon", "grp"), None),
        P(("lon", "grp")),
        P(("lon", "grp")),
        P(("lon", "grp")),
        P("lon", None, None),
        P("lon", None, None),
        P("lon", None, None),
        P("lon", None, None),
        P(),
        P(),
    )
    return jax.shard_map(
        on_device,
        mesh=mesh,
        in_specs=placed,
        out_specs=(
            P("lon", None, None),
            P("lon", None, None),
            P("lon", None, None),
            P(("lon", "grp")),
            P("lon", None, None),
            P(),
        ),
        check_vma=False,
    )
```

```python
import functools
import math

import jax
import jax.numpy as jnp
from jax import lax
from jax.experimental import pallas as pl
from jax.experimental.pallas import tpu as pltpu
from jax.sharding import PartitionSpec as P

EPSILON = 1e-06
MESH = pl.DeviceIdType.MESH
F32 = jnp.float32
BF16 = jnp.bfloat16
LANES = 128
META = 16
TILE = 16
CHUNK_BLOCKS = 4
NT = (((1,), (1,)), ((), ()))
NN = (((1,), (0,)), ((), ()))


def dot(a, b, dims=NN):
    return lax.dot_general(a, b, dims, preferred_element_type=F32)


def kernel(
    cfg,
    stencil_ref,
    scalar_ref,
    sector_hbm,
    block_hbm,
    offset_hbm,
    left_hbm,
    w_ref,
    v_ref,
    resid_ref,
    sr_ref,
    back_ref,
    home_ref,
    coef_ref,
    msg,
    rays,
    halo,
    psend,
    vhi,
    vlo,
    wx,
    rr,
    ret_send,
    ret_recv,
    a_send,
    a_recv,
    y_send,
    y_recv,
    c_send,
    c_recv,
    d_send,
    d_recv,
    h_send,
    h_recv,
    hy_send,
    hy_recv,
    hc_send,
    hc_recv,
    hd_send,
    hd_recv,
    r_send,
    r_recv,
    sector_ref,
    block_ref,
    offset_ref,
    left_ref,
    l_sem,
):
    n, groups, capp, ray_count, lat, depth, ratio, rows_total, cells_total = cfg
    me = lax.axis_index("lon")
    g = lax.axis_index("grp")
    gy = lax.rem(g + 2, 4)
    gc = g + 1 - 2 * lax.rem(g, 2)
    right = lax.rem(me + 1, n)
    left = lax.rem(me + n - 1, n)
    share = lat // groups
    q0 = pl.multiple_of(g * share, share)
    qy0 = pl.multiple_of(gy * share, share)
    k0 = stencil_ref[0]
    k1 = stencil_ref[1]
    k2 = stencil_ref[2]
    diag = 2.0 * (k0 + k1 + k2) + stencil_ref[3]
    alpha = scalar_ref[0]

    loads = [
        pltpu.make_async_copy(src, dst, l_sem.at[i])
        for i, (src, dst) in enumerate(
            (
                (sector_hbm, sector_ref),
                (block_hbm, block_ref),
                (offset_hbm, offset_ref),
                (left_hbm, left_ref),
            )
        )
    ]
    for load in loads:
        load.start()

    barrier = pltpu.get_barrier_semaphore()

    def greet(d, carry):
        pl.semaphore_signal(
            barrier, inc=1, device_id=(lax.rem(me + d, n), g), device_id_type=MESH
        )
        return carry

    lax.fori_loop(1, n, greet, 0)
    pl.semaphore_signal(barrier, inc=1, device_id=(me, gy), device_id_type=MESH)
    pl.semaphore_signal(barrier, inc=1, device_id=(me, gc), device_id_type=MESH)

    pl.semaphore_wait(barrier, n + 1)

    own = pl.ds(q0, share)
    sources = [
        (v_ref.at[1, own], right),
        (v_ref.at[0, own], left),
        (psend.at[1], right),
        (psend.at[0], left),
    ]
    halo_copies = [
        pltpu.make_async_remote_copy(
            src, halo.at[i, own], h_send.at[i], h_recv.at[i],
            device_id=(peer, g), device_id_type=MESH,
        )
        for i, (src, peer) in enumerate(sources)
    ]
    for copy in halo_copies[:2]:
        copy.start()

    for load in loads:
        load.wait()

    target = sector_ref[...].astype(F32)
    block = block_ref[...].astype(F32)
    offset = offset_ref[...].astype(F32)
    resid = left_ref[...]
    sector_rows = -(-n // 16) * 16
    sector_iota = lax.broadcasted_iota(jnp.int32, (sector_rows, ray_count), 0).astype(F32)
    hits = (sector_iota == target).astype(F32)
    before = lax.broadcasted_iota(jnp.int32, (ray_count, ray_count), 0) < lax.broadcasted_iota(
        jnp.int32, (ray_count, ray_count), 1
    )
    rank_all = dot(hits.astype(BF16), jnp.where(before, 1.0, 0.0).astype(BF16))
    slot = target * capp + jnp.sum(hits * rank_all, axis=0, keepdims=True)

    offset_col = jnp.transpose(jnp.broadcast_to(offset, (8, ray_count)))[:, 0:1].astype(jnp.int32)
    turned = w_ref[...].astype(F32)
    for bit in range(7):
        on = lax.rem(offset_col // (1 << bit), 2) == 1
        turned = jnp.where(on, pltpu.roll(turned, 1 << bit, 1), turned)
    turned = turned.astype(BF16)
    block_high = jnp.floor(block * (1.0 / 32))
    offset_high = jnp.floor(offset * (1.0 / 32))
    fields = jnp.concatenate(
        [
            block_high,
            block - 32.0 * block_high,
            offset_high,
            offset - 32.0 * offset_high,
            resid,
            jnp.zeros((META - 5, ray_count), F32),
        ],
        axis=0,
    ).astype(BF16)
    slot_iota = lax.broadcasted_iota(jnp.int32, (capp, ray_count), 0)

    def chosen(s):
        return jnp.where(slot == (slot_iota + s * capp).astype(F32), 1.0, 0.0).astype(BF16)

    def fill(s, carry):
        picked = chosen(s)
        msg[s, :capp, :] = dot(picked, turned).astype(BF16)
        msg[s, capp:, :] = dot(fields, picked, NT).astype(BF16)
        return carry

    lax.fori_loop(0, n, fill, 0)
    rays[g, me] = msg[me]

    def route(d):
        peer = lax.rem(me + d, n)
        return pltpu.make_async_remote_copy(
            msg.at[peer], rays.at[g, me], a_send.at[d], a_recv.at[d],
            device_id=(peer, g), device_id_type=MESH,
        )

    def route_start(d, carry):
        route(d).start()
        return carry

    lax.fori_loop(1, n, route_start, 0)

    lane = lax.broadcasted_iota(jnp.int32, (TILE, depth), 1)
    first_lane = lane == 0
    last_lane = lane == depth - 1

    def planar(ref, layer, start):
        low = ref[layer, pl.ds(pl.multiple_of(jnp.maximum(start - 8, 0), 8), 8), :]
        low = low * jnp.where(start > 0, 1.0, 0.0)
        high = ref[layer, pl.ds(pl.multiple_of(jnp.minimum(start + TILE, lat - 8), 8), 8), :]
        high = high * jnp.where(start + TILE < lat, 1.0, 0.0)
        mid = ref[layer, pl.ds(start, TILE), :]
        tall = jnp.concatenate([low, mid, high], axis=0)
        rows = TILE + 16
        along_lat = pltpu.roll(tall, 1, 0)[8 : 8 + TILE] + pltpu.roll(tall, rows - 1, 0)[8 : 8 + TILE]
        along_depth = jnp.where(first_lane, 0.0, pltpu.roll(mid, 1, 1)) + jnp.where(
            last_lane, 0.0, pltpu.roll(mid, depth - 1, 1)
        )
        return diag * mid - k1 * along_lat - k2 * along_depth, mid

    for layer in range(2):

        def outer(t, carry, layer=layer):
            start = pl.multiple_of(q0 + t * TILE, TILE)
            plane, _ = planar(v_ref, layer, start)
            other = v_ref[1 - layer, pl.ds(start, TILE), :]
            psend[layer, pl.ds(pl.multiple_of(t * TILE, TILE), TILE), :] = (
                ratio * (plane - k0 * other) - alpha * resid_ref[layer, pl.ds(start, TILE), :]
            )
            return carry

        lax.fori_loop(0, share // TILE, outer, 0)

    for copy in halo_copies[2:]:
        copy.start()

    def along_y(d):
        src = rays.at[g, lax.rem(me - d + n, n)]
        return pltpu.make_async_remote_copy(
            src, src, y_send.at[d], y_recv.at[d], device_id=(me, gy), device_id_type=MESH
        )

    def along_c(d):
        src = rays.at[g, lax.rem(me - d + n, n)]
        return pltpu.make_async_remote_copy(
            src, src, c_send.at[d], c_recv.at[d], device_id=(me, gc), device_id_type=MESH
        )

    def along_d(d):
        src = rays.at[gy, lax.rem(me - d + n, n)]
        return pltpu.make_async_remote_copy(
            src, src, d_send.at[d], d_recv.at[d], device_id=(me, gc), device_id_type=MESH
        )

    along_y(0).start()
    along_c(0).start()

    def pass_on(d, carry):
        route(d).wait_recv()
        along_y(d).start()
        along_c(d).start()
        return carry

    lax.fori_loop(1, n, pass_on, 0)

    def split(t, carry):
        rows = pl.ds(pl.multiple_of(t * TILE, TILE), TILE)
        for layer in range(2):
            x = v_ref[layer, rows, :]
            high = x.astype(BF16)
            target_rows = pl.ds(pl.multiple_of(layer * lat + t * TILE, TILE), TILE)
            vhi[target_rows, :] = high
            vlo[target_rows, :] = (x - high.astype(F32)).astype(BF16)
            back_ref[layer, rows, :] = jnp.zeros((TILE, depth), F32)
        return carry

    lax.fori_loop(0, lat // TILE, split, 0)

    for layer in range(2):

        def inner(t, carry, layer=layer):
            start = pl.multiple_of(t * TILE, TILE)
            rows = pl.ds(start, TILE)
            plane, _ = planar(v_ref, layer, start)
            sr_ref[layer, rows, :] = (
                ratio * (plane - k0 * v_ref[1 - layer, rows, :])
                - alpha * resid_ref[layer, rows, :]
            )
            return carry

        lax.fori_loop(0, lat // TILE, inner, 0)

    def pass_again(d, carry):
        along_y(d).wait_recv()
        along_d(d).start()
        return carry

    lax.fori_loop(0, n, pass_again, 0)

    def piece_to(rows, sends, recvs, to):
        return [
            pltpu.make_async_remote_copy(
                halo.at[i, rows], halo.at[i, rows], sends.at[i], recvs.at[i],
                device_id=(me, to), device_id_type=MESH,
            )
            for i in range(4)
        ]

    hy = piece_to(own, hy_send, hy_recv, gy)
    hc = piece_to(own, hc_send, hc_recv, gc)
    hd = piece_to(pl.ds(qy0, share), hd_send, hd_recv, gc)

    def halo_on(first):
        for i in (first, first + 1):
            halo_copies[i].wait_recv()
            hy[i].start()
            hc[i].start()

    def halo_again(first):
        for i in (first, first + 1):
            hy[i].wait_recv()
            hd[i].start()

    halo_on(0)

    def settle(d, carry):
        along_c(d).wait_recv()
        along_d(d).wait_recv()
        return carry

    lax.fori_loop(0, n, settle, 0)

    per_group = n // CHUNK_BLOCKS
    chunk = CHUNK_BLOCKS * capp
    cells = 2 * lat
    cell_tile = math.gcd(cells, 256)
    cell_iota = lax.broadcasted_iota(jnp.int32, (cell_tile, chunk), 0)
    spot = lax.broadcasted_iota(jnp.int32, (capp, LANES), 1)

    def ray_chunk(c, square):
        source_group = c // per_group
        base = lax.rem(c, per_group) * CHUNK_BLOCKS
        block_rows = []
        resid_rows = []
        for i in range(CHUNK_BLOCKS):
            meta = rays[source_group, base + i, capp:, :].astype(F32)
            block_rows.append(meta[0:1] * 32.0 + meta[1:2])
            resid_rows.append(meta[4:5])
            start = jnp.broadcast_to(meta[2:3] * 32.0 + meta[3:4], (8, capp))
            start_col = jnp.transpose(start)[:, 0:1].astype(jnp.int32)
            weights = rays[source_group, base + i, :capp, :].astype(F32)
            for j in range(depth // LANES):
                where = spot + (j * LANES) - start_col
                inside = (where >= 0) & (where < LANES)
                wx[i * capp : (i + 1) * capp, j * LANES : (j + 1) * LANES] = jnp.where(
                    inside, weights, 0.0
                ).astype(BF16)
        block_row = jnp.concatenate(block_rows, axis=1).astype(jnp.int32)
        resid_row = jnp.concatenate(resid_rows, axis=1)

        def product(t, total):
            rows = pl.ds(pl.multiple_of(t * cell_tile, cell_tile), cell_tile)
            found = dot(vhi[rows, :], wx[...], NT) + dot(vlo[rows, :], wx[...], NT)
            hit = (cell_iota + t * cell_tile) == block_row
            return total + jnp.sum(jnp.where(hit, found, 0.0), axis=0, keepdims=True)

        path = lax.fori_loop(0, cells // cell_tile, product, jnp.zeros((1, chunk), F32))
        raw = ratio * path - alpha * resid_row
        for i in range(CHUNK_BLOCKS):
            rr[source_group * n + base + i] = jnp.broadcast_to(
                raw[:, i * capp : (i + 1) * capp], (8, capp)
            )
        raw_high = raw.astype(BF16).astype(F32)
        raw_low = raw - raw_high

        def spread(t, carry):
            layer = t * cell_tile // lat
            rows = pl.ds(pl.multiple_of(lax.rem(t * cell_tile, lat), cell_tile), cell_tile)
            hit = (cell_iota + t * cell_tile) == block_row
            back_ref[layer, rows, :] += dot(
                jnp.where(hit, raw_high, 0.0).astype(BF16), wx[...]
            ) + dot(jnp.where(hit, raw_low, 0.0).astype(BF16), wx[...])
            return carry

        lax.fori_loop(0, cells // cell_tile, spread, 0)
        return square + raw * raw

    chunks = groups * per_group
    square = jnp.zeros((1, chunk), F32)
    bounds = [chunks * i // 8 for i in (0, 1, 4, 7, 8)]
    for i, step in enumerate((lambda: halo_on(2), lambda: halo_again(0), lambda: halo_again(2), None)):
        square = lax.fori_loop(bounds[i], bounds[i + 1], ray_chunk, square)
        if step is not None:
            step()
    ray_square = jnp.sum(square)
    for i in range(4):
        hc[i].wait_recv()
        hd[i].wait_recv()

    def fold(x):
        return jnp.sum(x.reshape(TILE // 8, 8, depth), axis=0)

    zero = jnp.zeros((8, depth), F32)
    smooth_square = zero
    for layer in range(2):

        def forward(t, total, layer=layer):
            start = pl.multiple_of(t * TILE, TILE)
            rows = pl.ds(start, TILE)
            raw = sr_ref[layer, rows, :] - (ratio * k0) * halo[layer, rows, :]
            sr_ref[layer, rows, :] = raw
            return total + fold(raw * raw)

        smooth_square = lax.fori_loop(0, lat // TILE, forward, smooth_square)

    totals = (zero, zero, zero)
    for layer in range(2):

        def transposed(t, totals, layer=layer):
            start = pl.multiple_of(t * TILE, TILE)
            rows = pl.ds(start, TILE)
            plane, _ = planar(sr_ref, layer, start)
            x = v_ref[layer, rows, :]
            outside = halo[2 + layer, rows, :] - (ratio * k0) * x
            value = back_ref[layer, rows, :] + plane - k0 * (outside + sr_ref[1 - layer, rows, :])
            back_ref[layer, rows, :] = value
            return (
                totals[0] + fold(value * value),
                totals[1] + fold(value * x),
                totals[2] + fold(x * x),
            )

        totals = lax.fori_loop(0, lat // TILE, transposed, totals)

    sub = lax.broadcasted_iota(jnp.int32, (8, LANES), 0)
    col = lax.broadcasted_iota(jnp.int32, (8, LANES), 1)
    numbers = [ray_square + jnp.sum(smooth_square)] + [jnp.sum(x) for x in totals]
    sums = jnp.zeros((8, LANES), F32)
    for i, number in enumerate(numbers):
        sums = jnp.where(col == i, number, sums)

    def answer(s, carry):
        ret_send[s] = jnp.where(sub == 0, rr[g * n + s], sums)
        return carry

    lax.fori_loop(0, n, answer, 0)
    ret_recv[me] = ret_send[me]

    def give_back(d):
        peer = lax.rem(me + d, n)
        return pltpu.make_async_remote_copy(
            ret_send.at[peer], ret_recv.at[me], r_send.at[d], r_recv.at[d],
            device_id=(peer, g), device_id_type=MESH,
        )

    def give_start(d, carry):
        give_back(d).start()
        return carry

    def give_wait(d, carry):
        give_back(d).wait_recv()
        return carry

    lax.fori_loop(1, n, give_start, 0)
    lax.fori_loop(1, n, give_wait, 0)

    def collect(s, carry):
        total, home = carry
        tile = ret_recv[s]
        one = tile.astype(BF16).astype(F32)
        two = (tile - one).astype(BF16).astype(F32)
        three = tile - one - two
        stack = jnp.concatenate([one, two, three, jnp.zeros((8, LANES), F32)], axis=0).astype(BF16)
        got = dot(stack, chosen(s))
        return total + tile, home + (got[0:8] + got[8:16] + got[16:24])

    total, home = lax.fori_loop(
        0, n, collect, (jnp.zeros((8, LANES), F32), jnp.zeros((8, ray_count), F32))
    )

    def number_of(i):
        return jnp.broadcast_to(total[1:2, i : i + 1], (8, LANES))

    rho_bar = scalar_ref[1]
    phi_bar = scalar_ref[2]
    beta = jnp.sqrt(number_of(0) / rows_total + EPSILON)
    scale = 1.0 / (beta * ratio)
    spread_sum = (
        scale * scale * number_of(1)
        - 2.0 * (scale * beta) * number_of(2)
        + beta * beta * number_of(3)
    )
    alpha_new = jnp.sqrt(jnp.maximum(spread_sum, 0.0) / cells_total + EPSILON)
    rho = jnp.sqrt(rho_bar * rho_bar + beta * beta)
    cosine = rho_bar / rho
    sine = beta / rho
    results = [
        alpha_new,
        beta,
        -cosine * alpha_new,
        sine * phi_bar,
        cosine * phi_bar / rho,
        sine * alpha_new / rho,
        scale / alpha_new,
        beta / alpha_new,
        1.0 / beta,
    ]
    tile = jnp.zeros((8, LANES), F32)
    for i, result in enumerate(results):
        tile = jnp.where(col == i, result, tile)
    coef_ref[...] = tile
    home_ref[...] = home / beta[:, 0:1]

    def finish(d, carry):
        route(d).wait_send()
        give_back(d).wait_send()
        return carry

    lax.fori_loop(1, n, finish, 0)

    def finish_all(d, carry):
        along_y(d).wait_send()
        along_c(d).wait_send()
        along_d(d).wait_send()
        return carry

    lax.fori_loop(0, n, finish_all, 0)
    for copy in halo_copies + hy + hc + hd:
        copy.wait_send()


def update(coef, raw, back, v, search, model, model_new, search_new, dir_new, smooth_new):
    def value(i):
        return coef[0:1, i : i + 1]

    for layer in range(2):
        turned = back[layer] * value(6) - v[layer] * value(7)
        dir_new[layer] = turned
        search_new[layer] = turned - value(5) * search[layer]
        model_new[layer] = model[layer] + value(4) * search[layer]
        smooth_new[layer] = raw[layer] * value(8)


def on_device(
    ray_weights,
    ray_sector,
    ray_block,
    ray_offset,
    ray_resid,
    smooth_resid,
    model_dir,
    search_dir,
    model,
    stencil_coeffs,
    lsqr_scalars,
):
    n = lax.axis_size("lon")
    groups = lax.axis_size("grp")
    ray_count = ray_weights.shape[0]
    lon_cells, lat, depth = model_dir.shape
    assert lon_cells == 2 and groups == 4 and n % CHUNK_BLOCKS == 0
    capacity = 2 * ray_count // n
    capp = -(-capacity // LANES) * LANES
    assert capp == LANES
    cells_total = lon_cells * lat * depth * n
    rows_total = ray_count * n * groups + cells_total
    ratio = math.sqrt(rows_total / cells_total)
    field = jax.ShapeDtypeStruct((2, lat, depth), F32)
    vmem = pl.BlockSpec(memory_space=pltpu.VMEM)
    dma = pltpu.SemaphoreType.DMA
    cfg = (n, groups, capp, ray_count, lat, depth, ratio, rows_total, cells_total)
    smooth_raw, back, home, coef = pl.pallas_call(
        functools.partial(kernel, cfg),
        out_shape=(
            field,
            field,
            jax.ShapeDtypeStruct((8, ray_count), F32),
            jax.ShapeDtypeStruct((8, LANES), F32),
        ),
        in_specs=[pl.BlockSpec(memory_space=pltpu.SMEM)] * 2 + [pl.BlockSpec(memory_space=pl.ANY)] * 4 + [vmem] * 3,
        out_specs=(vmem,) * 4,
        scratch_shapes=[
            pltpu.VMEM((n, capp + META, LANES), BF16),
            pltpu.VMEM((groups, n, capp + META, LANES), BF16),
            pltpu.VMEM((4, lat, depth), F32),
            pltpu.VMEM((2, lat // groups, depth), F32),
            pltpu.VMEM((2 * lat, depth), BF16),
            pltpu.VMEM((2 * lat, depth), BF16),
            pltpu.VMEM((CHUNK_BLOCKS * capp, depth), BF16),
            pltpu.VMEM((groups * n, 8, capp), F32),
            pltpu.VMEM((n, 8, LANES), F32),
            pltpu.VMEM((n, 8, LANES), F32),
        ]
        + [dma((n,))] * 8
        + [dma((4,))] * 8
        + [dma((n,))] * 2
        + [pltpu.VMEM((1, ray_count), jnp.int32)] * 3
        + [pltpu.VMEM((1, ray_count), F32), dma((4,))],
        compiler_params=pltpu.CompilerParams(
            collective_id=0, has_side_effects=True, vmem_limit_bytes=48 * 1024 * 1024
        ),
        cost_estimate=pl.CostEstimate(
            flops=20_000_000_000, bytes_accessed=8_000_000, transcendentals=0
        ),
    )(
        stencil_coeffs,
        lsqr_scalars,
        ray_sector.reshape(1, ray_count),
        ray_block.reshape(1, ray_count),
        ray_offset.reshape(1, ray_count),
        ray_resid.reshape(1, ray_count),
        ray_weights,
        model_dir,
        smooth_resid,
    )

    lat_block = math.gcd(lat, 64)
    whole = pl.BlockSpec((8, LANES), lambda t: (0, 0))
    part = pl.BlockSpec((2, lat_block, depth), lambda t: (0, t, 0))
    model_new, search_new, dir_new, smooth_new = pl.pallas_call(
        update,
        grid=(lat // lat_block,),
        out_shape=(field,) * 4,
        in_specs=[whole] + [part] * 5,
        out_specs=(part,) * 4,
        compiler_params=pltpu.CompilerParams(vmem_limit_bytes=24 * 1024 * 1024),
        cost_estimate=pl.CostEstimate(
            flops=10_000_000, bytes_accessed=18_874_368, transcendentals=0
        ),
    )(coef, smooth_raw, back, model_dir, search_dir, model)
    return (model_new, search_new, dir_new, home[0], smooth_new, coef[0, :4])


def solution(mesh):
    placed = (
        P(("lon", "grp"), None),
        P(("lon", "grp"), None),
        P(("lon", "grp")),
        P(("lon", "grp")),
        P(("lon", "grp")),
        P("lon", None, None),
        P("lon", None, None),
        P("lon", None, None),
        P("lon", None, None),
        P(),
        P(),
    )
    return jax.shard_map(
        on_device,
        mesh=mesh,
        in_specs=placed,
        out_specs=(
            P("lon", None, None),
            P("lon", None, None),
            P("lon", None, None),
            P(("lon", "grp")),
            P("lon", None, None),
            P(),
        ),
        check_vma=False,
    )
```
